128 devices in a mesh: gx: 8 (over z, core), gy: 16 (over x, y).
Axes of the slice: x: 4, y: 4, z: 4, core: 2. Of those that a mesh axis runs over, the one named last changes fastest.
Arguments:
- prior_draws: bfloat16 [8, 16, 512, 256], P('gx', 'gy'), may hold values from -8 to 8
- cond_factors: bfloat16 [4, 8, 16, 8, 512, 512], P(None, 'gx', 'gy'), may hold values from -0.0625 to 0.0625
- chol_factors: bfloat16 [4, 8, 16, 512, 512], P(None, 'gx', 'gy'), may hold values from -0.25 to 0.25
- noise: bfloat16 [4, 8, 16, 512, 256], P(None, 'gx', 'gy'), may hold values from -6 to 6
- neighbours: int32 [4, 8, 16, 8], P(None, 'gx', 'gy'), may hold values from 0 to 639, as said below
- block_slot: int32 [640], replicated, may hold values from 0 to 639, as said below
Outputs:
- samples: bfloat16 [4, 8, 16, 512, 256], P(None, 'gx', 'gy')
The draws below stay inside these ranges and needn't reach their ends.
Inputs may be any that keep to these rules, and one draw needn't show every extreme that they name: `block_slot`: A permutation of 0 to 639. `neighbours`: the K blocks of entry [l, i, j] are distinct, lie at level l, and are owned by devices with gx index i or gy index j (the owner itself may be one).
All inputs are finite; a program needn't handle non-finite values.
Results may differ from the reference program's by a relative error of at most 0.0045.
Values may be sent and summed in bfloat16 or wider, within the bound.
No kernel may reach another device: no remote copies, remote signals or barrier semaphores. Data moves between devices by JAX's collectives and lax.ppermute only.
A program may use at most 128 MiB of HBM per device.

```python
import jax
import jax.numpy as jnp
from jax import lax

B = 512
R = 256
K = 8
LEVELS = 5
LW = 4
N_GX = 8
N_GY = 16


def slot_table(key):
    return jax.random.permutation(key, LEVELS * N_GX * N_GY).astype(jnp.int32)


def draw_block_slot(key, part):
    return slot_table(key)


def draw_neighbours(key, part):
    slots = slot_table(key)
    key = jax.random.fold_in(key, 7)
    devices = N_GX * N_GY
    total = LEVELS * devices
    candidates = N_GX + N_GY - 1
    inverse = jnp.zeros((total,), jnp.int32).at[slots].set(jnp.arange(total, dtype=jnp.int32))
    scores = jax.random.randint(key, ((LEVELS - 1) * devices, candidates), 0, 2 ** 20)
    scores = scores * candidates + jnp.arange(candidates, dtype=jnp.int32)[None, :]
    chosen = jnp.argsort(scores, axis=1)[:, :K].astype(jnp.int32)
    entry = jnp.arange((LEVELS - 1) * devices, dtype=jnp.int32)[:, None]
    device = entry % devices
    level = entry // devices
    row_index = device // N_GY
    col_index = device % N_GY
    row_device = row_index * N_GY + chosen
    other_row = chosen - N_GY
    other_row = other_row + (other_row >= row_index).astype(jnp.int32)
    col_device = other_row * N_GY + col_index
    source = jnp.where(chosen < N_GY, row_device, col_device)
    found = inverse[level * devices + source]
    return found.reshape(LEVELS - 1, N_GX, N_GY, K)


def steps_of(key, shape, cuts, low, top_value):
    def one(axis_at, parts):
        heights = jax.random.uniform(jax.random.fold_in(jax.random.fold_in(key, 6), axis_at), (parts,), jnp.float32, low / len(cuts), top_value / len(cuts))
        return jnp.repeat(jnp.exp(heights), shape[axis_at] // parts).reshape((-1,) + (1,) * (len(shape) - axis_at - 1))

    factor_of = one(*cuts[0])
    for cut in cuts[1:]:
        factor_of = factor_of * one(*cut)
    return factor_of


def gaussian(own_key, dims, scale, limit, shards=(), kind=jnp.bfloat16):
    factor_of = steps_of(own_key, dims, shards, -0.22, 0.18) if shards else 1.0
    entries = jax.random.normal(own_key, dims, jnp.float32) * scale * factor_of
    return jnp.minimum(jnp.maximum(entries, -limit), limit).astype(kind)


def setup_inputs(seed: int = 0) -> dict:
    keys = jax.random.split(jax.random.key(seed), 7)
    return {
        "prior_draws": gaussian(keys[0], (N_GX, N_GY, B, R), 1.4, 8.0, ((0, 8), (1, 16))),
        "cond_factors": gaussian(keys[1], (LW, N_GX, N_GY, K, B, B), (2 * K * B) ** -0.5, 0.0625, ((1, 8), (2, 16))),
        "chol_factors": gaussian(keys[2], (LW, N_GX, N_GY, B, B), B ** -0.5, 0.25, ((1, 8), (2, 16))),
        "noise": gaussian(keys[3], (LW, N_GX, N_GY, B, R), 1.0, 6.0, ((1, 8), (2, 16))),
        "neighbours": draw_neighbours(jax.random.fold_in(keys[6], 71), 0),
        "block_slot": draw_block_slot(jax.random.fold_in(keys[6], 71), 0),
    }


def reference(prior_draws, cond_factors, chol_factors, noise, neighbours, block_slot):
    devices = N_GX * N_GY
    previous = prior_draws.reshape(devices, B, R)
    sources = (block_slot[neighbours] % devices).astype(jnp.int32).reshape(LW, devices, K)
    levels_out = []
    for level in range(LW):
        factors = cond_factors[level].reshape(devices, K, B, B)
        cholesky = chol_factors[level].reshape(devices, B, B)
        innovations = noise[level].reshape(devices, B, R)

        def one_block(items, previous=previous):
            factor_d, chol_d, noise_d, source_d = items
            picked = previous[source_d]
            mean = jnp.einsum("kbc,kcr->br", factor_d.astype(jnp.float32), picked.astype(jnp.float32))
            own = jnp.dot(chol_d, noise_d, preferred_element_type=jnp.float32)
            return (mean + own).astype(jnp.bfloat16)

        previous = lax.map(one_block, (factors, cholesky, innovations, sources[level]))
        levels_out.append(previous.reshape(N_GX, N_GY, B, R))
    return jnp.stack(levels_out)
```

```python
import functools

import jax
import jax.numpy as jnp
from jax import lax
from jax.experimental import pallas as pl
from jax.experimental.pallas import tpu as pltpu
from jax.sharding import PartitionSpec as P

AXES = ("gx", "gy")
SIDE = 4


def pairs(move):
    out = []
    for z in range(SIDE):
        for c in range(2):
            for x in range(SIDE):
                for y in range(SIDE):
                    x2, y2, z2, c2 = move(x, y, z, c)
                    target = ((z2 % SIDE) * 2 + c2) * SIDE * SIDE + (x2 % SIDE) * SIDE + y2 % SIDE
                    out.append(((z * 2 + c) * SIDE * SIDE + x * SIDE + y, target))
    return out


def first(step):
    return pairs(lambda x, y, z, c: (x + step, y, z, c) if c == 0 else (x, y + step, z, c))


def second(step):
    return pairs(lambda x, y, z, c: (x, y + step, z, c) if c == 0 else (x + step, y, z, c))


def along_z(step):
    return pairs(lambda x, y, z, c: (x, y, z + step, c))


OTHER = pairs(lambda x, y, z, c: (x, y, z, 1 - c))


def send(value, route):
    return lax.ppermute(value, AXES, route)


def level_kernel(level, where_ref, *refs):
    sources = refs[:10]
    own_f, other_f, own_c, other_c, noise_ref, out_ref, factor, chol, picked, total, sem_f, sem_c = refs[10:]
    copies = []
    for k in range(8):
        for j, ref in enumerate((own_f, other_f)):
            copies.append(pltpu.make_async_copy(ref.at[level, k], factor.at[j, k], sem_f.at[j, k]))
    for j, ref in enumerate((own_c, other_c)):
        copies.append(pltpu.make_async_copy(ref.at[level], chol.at[j], sem_c.at[j]))
    for copy in copies[16:] + copies[:16]:
        copy.start()

    for j in range(2):
        copies[16 + j].wait()
        total[j] = jnp.dot(chol[j], noise_ref[j], preferred_element_type=jnp.float32)

    def step(k, carry):
        for j, ref in enumerate((own_f, other_f)):
            code = where_ref[level, j, k]
            which = code // 8
            part = code % 8
            for r, source in enumerate(sources):
                @pl.when(which == r)
                def _():
                    picked[j] = source[part]
            pltpu.make_async_copy(ref.at[level, k], factor.at[j, k], sem_f.at[j, k]).wait()
            total[j] += jnp.dot(factor[j, k], picked[j], preferred_element_type=jnp.float32)
        return carry

    lax.fori_loop(0, 8, step, 0)
    out_ref[...] = total[...].astype(out_ref.dtype)


def level_call(level, where, sources, own_f, other_f, own_c, other_c, noise):
    vmem = pl.BlockSpec(memory_space=pltpu.VMEM)
    anywhere = pl.BlockSpec(memory_space=pl.ANY)
    rows = own_f.shape[-1]
    columns = noise.shape[-1]
    return pl.pallas_call(
        functools.partial(level_kernel, level),
        out_shape=jax.ShapeDtypeStruct((2, rows, columns), jnp.bfloat16),
        in_specs=[pl.BlockSpec(memory_space=pltpu.SMEM)] + [vmem] * 10 + [anywhere] * 4 + [vmem],
        out_specs=vmem,
        scratch_shapes=[
            pltpu.VMEM((2, 8, rows, rows), jnp.bfloat16),
            pltpu.VMEM((2, rows, rows), jnp.bfloat16),
            pltpu.VMEM((2, rows, columns), jnp.bfloat16),
            pltpu.VMEM((2, rows, columns), jnp.float32),
            pltpu.SemaphoreType.DMA((2, 8)),
            pltpu.SemaphoreType.DMA((2,)),
        ],
        compiler_params=pltpu.CompilerParams(vmem_limit_bytes=28 * 1024 * 1024),
        cost_estimate=pl.CostEstimate(
            flops=2 * 18 * rows * rows * columns, bytes_accessed=18 * rows * rows * 2, transcendentals=0
        ),
    )(where, *sources, own_f, other_f, own_c, other_c, noise)


def body(prior_draws, cond_factors, chol_factors, noise, neighbours, block_slot):
    my_gx = lax.axis_index("gx")
    my_gy = lax.axis_index("gy")
    z, core = my_gx // 2, my_gx % 2
    x, y = my_gy // SIDE, my_gy % SIDE
    half = prior_draws.shape[-1] // 2
    low = core == 0

    def mine(block):
        return jnp.where(low, block[..., :half], block[..., half:])

    def others(block):
        return jnp.where(low, block[..., half:], block[..., :half])

    prior = prior_draws[0, 0]
    draws = jnp.stack([mine(prior), send(others(prior), OTHER)])
    own_f = cond_factors[:, 0, 0]
    other_f = send(own_f, OTHER)
    own_c = chol_factors[:, 0, 0]
    other_c = send(own_c, OTHER)
    own_noise = noise[:, 0, 0]
    noises = jnp.stack([mine(own_noise), send(others(own_noise), OTHER)], axis=1)
    own_n = neighbours[:, 0, 0]
    both_n = jnp.stack([own_n, send(own_n, OTHER)], axis=1)

    device = block_slot[both_n] % (2 * SIDE**3)
    row, col = device // (SIDE * SIDE), device % (SIDE * SIDE)
    same_core = row % 2 == core
    j = jnp.arange(2, dtype=jnp.int32)[None, :, None]
    my_row = z * 2 + jnp.where(j == 0, core, 1 - core)
    dx, dy = (col // SIDE - x) % SIDE, (col % SIDE - y) % SIDE
    dz = (row // 2 - z) % SIDE
    d1, d2 = jnp.where(low, dx, dy), jnp.where(low, dy, dx)
    place = lambda d: jnp.where(d == 0, 0, jnp.where(d == 3, 1, jnp.where(d == 1, 2, 3)))
    p1, p2, p3 = place(d1), place(d2), place(dz)
    in_row = jnp.where(p2 == 0, p1 * 8 + j, (3 + p2) * 8 + p1 * 2 + j)
    other_j = jnp.where(same_core, 0, 1)
    in_col = jnp.where(p3 == 0, 0, 6 + p3) * 8 + other_j
    where = jnp.where(row == my_row, in_row, in_col).astype(jnp.int32)

    results = []
    for level in range(cond_factors.shape[0]):
        near = [send(draws, first(s)) for s in (1, -1, 2)]
        column = [send(draws, along_z(s)) for s in (1, -1, 2)]
        line = jnp.concatenate([draws] + near)
        far = [send(line, second(s)) for s in (1, -1, 2)]
        draws = level_call(
            level, where, [draws] + near + far + column, own_f, other_f, own_c, other_c, noises[level]
        )
        got = send(draws[1], OTHER)
        results.append(
            jnp.where(
                low,
                jnp.concatenate([draws[0], got], axis=-1),
                jnp.concatenate([got, draws[0]], axis=-1),
            )
        )
    return jnp.stack(results)[:, None, None]


def solution(mesh):
    in_specs = (
        P("gx", "gy", None, None),
        P(None, "gx", "gy", None, None, None),
        P(None, "gx", "gy", None, None),
        P(None, "gx", "gy", None, None),
        P(None, "gx", "gy", None),
        P(),
    )
    out_specs = P(None, "gx", "gy", None, None)
    return jax.shard_map(body, mesh=mesh, in_specs=in_specs, out_specs=out_specs, check_vma=False)
```

```python
import functools

import jax
import jax.numpy as jnp
from jax import lax
from jax.experimental import pallas as pl
from jax.experimental.pallas import tpu as pltpu
from jax.sharding import PartitionSpec as P

AXES = ("gx", "gy")
SIDE = 4
SOON = 9


def pairs(move):
    out = []
    for z in range(SIDE):
        for c in range(2):
            for x in range(SIDE):
                for y in range(SIDE):
                    x2, y2, z2, c2 = move(x, y, z, c)
                    target = ((z2 % SIDE) * 2 + c2) * SIDE * SIDE + (x2 % SIDE) * SIDE + y2 % SIDE
                    out.append(((z * 2 + c) * SIDE * SIDE + x * SIDE + y, target))
    return out


def first(step):
    return pairs(lambda x, y, z, c: (x + step, y, z, c) if c == 0 else (x, y + step, z, c))


def second(step):
    return pairs(lambda x, y, z, c: (x, y + step, z, c) if c == 0 else (x + step, y, z, c))


def along_z(step):
    return pairs(lambda x, y, z, c: (x, y, z + step, c))


OTHER = pairs(lambda x, y, z, c: (x, y, z, 1 - c))


def send(value, route):
    return lax.ppermute(value, AXES, route)


VMEM = pl.BlockSpec(memory_space=pltpu.VMEM)
SMEM = pl.BlockSpec(memory_space=pltpu.SMEM)
ANYWHERE = pl.BlockSpec(memory_space=pl.ANY)
HBM = pl.BlockSpec(memory_space=pltpu.HBM)


def noise_kernel(core_ref, chol_ref, noise_ref, mine_ref, others_ref):
    half = mine_ref.shape[-1]
    product = jnp.dot(chol_ref[0], noise_ref[0], preferred_element_type=jnp.float32)

    @pl.when(core_ref[0] == 0)
    def _():
        mine_ref[0] = product[:, :half]
        others_ref[0] = product[:, half:]

    @pl.when(core_ref[0] != 0)
    def _():
        mine_ref[0] = product[:, half:]
        others_ref[0] = product[:, :half]


def noise_call(core, chol, noise):
    levels, rows, columns = noise.shape
    half = columns // 2
    part = pl.BlockSpec((1, rows, half), lambda l: (l, 0, 0))
    shape = jax.ShapeDtypeStruct((levels, rows, half), jnp.float32)
    return pl.pallas_call(
        noise_kernel,
        grid=(levels,),
        out_shape=(shape, shape),
        in_specs=[
            SMEM,
            pl.BlockSpec((1, rows, rows), lambda l: (l, 0, 0)),
            pl.BlockSpec((1, rows, columns), lambda l: (l, 0, 0)),
        ],
        out_specs=(part, part),
        cost_estimate=pl.CostEstimate(
            flops=2 * levels * rows * rows * columns, bytes_accessed=levels * rows * rows * 4, transcendentals=0
        ),
    )(core, chol, noise)


def pick(which, part, sources, target):
    def tree(low, high):
        if high - low == 1:
            target[...] = sources[low][part]
            return
        middle = (low + high) // 2

        @pl.when(which < middle)
        def _():
            tree(low, middle)

        @pl.when(which >= middle)
        def _():
            tree(middle, high)

    tree(0, len(sources))


def stage_kernel(level, token_ref, own_f, other_f, factor, sems):
    copies = [
        pltpu.make_async_copy(ref.at[level], factor.at[j], sems.at[j]) for j, ref in enumerate((own_f, other_f))
    ]
    for copy in copies:
        copy.start()
    for copy in copies:
        copy.wait()


def stage_call(level, token, own_f, other_f):
    return pl.pallas_call(
        functools.partial(stage_kernel, level),
        out_shape=jax.ShapeDtypeStruct((2,) + own_f.shape[1:], own_f.dtype),
        in_specs=[ANYWHERE, HBM, HBM],
        out_specs=VMEM,
        scratch_shapes=[pltpu.SemaphoreType.DMA((2,))],
        compiler_params=pltpu.CompilerParams(vmem_limit_bytes=24 * 1024 * 1024),
        cost_estimate=pl.CostEstimate(
            flops=0, bytes_accessed=2 * own_f.size // own_f.shape[0] * 2, transcendentals=0
        ),
    )(token, own_f, other_f)


def level_kernel(level, count, where_ref, *refs):
    sources = refs[:count]
    mine_ref, theirs_ref, factor, out_ref, give_ref, picked = refs[count:]

    def step(t, carry):
        code = where_ref[level, t // 8, t % 8]
        pick(code // 8, code % 8, sources, picked.at[t // 8, t % 8])
        return carry

    lax.fori_loop(0, 16, step, 0)
    for j, terms in enumerate((mine_ref, theirs_ref)):
        total = terms[level]
        for k in range(8):
            total += jnp.dot(factor[j, k], picked[j, k], preferred_element_type=jnp.float32)
        out_ref[j] = total.astype(out_ref.dtype)
    give_ref[...] = out_ref[1]


def level_call(level, where, sources, mine, theirs, factor):
    rows, columns = mine.shape[-2:]
    return pl.pallas_call(
        functools.partial(level_kernel, level, len(sources)),
        out_shape=(
            jax.ShapeDtypeStruct((2, rows, columns), jnp.bfloat16),
            jax.ShapeDtypeStruct((rows, columns), jnp.bfloat16),
        ),
        in_specs=[SMEM] + [VMEM] * (len(sources) + 3),
        out_specs=(VMEM, VMEM),
        scratch_shapes=[pltpu.VMEM((2, 8, rows, columns), jnp.bfloat16)],
        compiler_params=pltpu.CompilerParams(vmem_limit_bytes=24 * 1024 * 1024),
        cost_estimate=pl.CostEstimate(
            flops=2 * 16 * rows * rows * columns, bytes_accessed=16 * rows * columns * 2, transcendentals=0
        ),
    )(where, *sources, mine, theirs, factor)


def body(prior_draws, cond_factors, chol_factors, noise, neighbours, block_slot):
    my_gx = lax.axis_index("gx")
    my_gy = lax.axis_index("gy")
    z, core = my_gx // 2, my_gx % 2
    x, y = my_gy // SIDE, my_gy % SIDE
    half = prior_draws.shape[-1] // 2
    low = core == 0

    prior = prior_draws[0, 0]
    mine = jnp.where(low, prior[:, :half], prior[:, half:])
    others = jnp.where(low, prior[:, half:], prior[:, :half])
    draws = jnp.stack([mine, send(others, OTHER)])

    own_n = neighbours[:, 0, 0]
    both_n = jnp.stack([own_n, send(own_n, OTHER)], axis=1)

    device = block_slot[both_n] % (2 * SIDE**3)
    row, col = device // (SIDE * SIDE), device % (SIDE * SIDE)
    j = jnp.arange(2, dtype=jnp.int32)[None, :, None]
    my_row = z * 2 + jnp.where(j == 0, core, 1 - core)
    dx, dy = (col // SIDE - x) % SIDE, (col % SIDE - y) % SIDE
    dz = (row // 2 - z) % SIDE
    d1, d2 = jnp.where(low, dx, dy), jnp.where(low, dy, dx)

    def place(d):
        return jnp.where(d == 0, 0, jnp.where(d == 3, 1, jnp.where(d == 1, 2, 3)))

    p1, p2, p3 = place(d1), place(d2), place(dz)
    in_row = jnp.where(
        p2 == 0,
        p1 * 8 + j,
        jnp.where(
            p1 > 0,
            (SOON - 1 + p2) * 8 + (p1 - 1) * 2 + j,
            jnp.where(p2 < 3, (3 + p2) * 8 + j, (SOON + j) * 8 + 6),
        ),
    )
    in_col = jnp.where(p3 == 0, 0, 5 + p3) * 8 + jnp.where(row % 2 == core, 0, 1)
    where = jnp.where(row == my_row, in_row, in_col).astype(jnp.int32)

    own_f = cond_factors[:, 0, 0]
    chol, innovations = chol_factors[:, 0, 0], noise[:, 0, 0]

    kept, given, got = [], [], []
    for level in range(cond_factors.shape[0]):
        near = [send(draws, first(s)) for s in (2, 1, -1)]
        if level == 0:
            held, held_f, where = lax.optimization_barrier((draws, own_f, where))
            other_f = send(held_f, OTHER)
        else:
            swapped = send(given[-1], OTHER)
            held, swapped = lax.optimization_barrier((draws, swapped))
            got.append(swapped)
        along = [send(held, second(s)) for s in (1, -1)]
        line = jnp.concatenate([near[1], near[2], near[0]])
        if level == 0:
            line, chol, innovations = lax.optimization_barrier((line, chol, innovations))
            own_terms, sent_terms = noise_call(core.reshape(1), chol, innovations)
            other_terms = send(sent_terms, OTHER)
        held, line = lax.optimization_barrier((held, line))
        far = [
            send(line, second(2)),
            send(jnp.concatenate([line, along[0][:1]]), second(1)),
            send(jnp.concatenate([line, along[1][1:]]), second(-1)),
        ]
        column = [send(held, along_z(s)) for s in (2, 1, -1)]
        factor = stage_call(level, line, own_f, other_f)
        sources = [draws, near[1], near[2], near[0]] + along + [column[1], column[2], column[0]]
        sources += [far[1], far[2], far[0]]
        draws, give = level_call(level, where, sources, own_terms, other_terms, factor)
        kept.append(draws[0])
        given.append(give)
    got.append(send(given[-1], OTHER))
    left = jnp.stack(kept)
    right = jnp.stack(got)
    whole = jnp.where(low, jnp.concatenate([left, right], axis=-1), jnp.concatenate([right, left], axis=-1))
    return whole[:, None, None]


def solution(mesh):
    in_specs = (
        P("gx", "gy", None, None),
        P(None, "gx", "gy", None, None, None),
        P(None, "gx", "gy", None, None),
        P(None, "gx", "gy", None, None),
        P(None, "gx", "gy", None),
        P(),
    )
    out_specs = P(None, "gx", "gy", None, None)
    return jax.shard_map(body, mesh=mesh, in_specs=in_specs, out_specs=out_specs, check_vma=False)
```

```python
import functools

import jax
import jax.numpy as jnp
from jax import lax
from jax.experimental import pallas as pl
from jax.experimental.pallas import tpu as pltpu
from jax.sharding import PartitionSpec as P

AXES = ("gx", "gy")
SIDE = 4
SOON = 9


def pairs(move):
    out = []
    for z in range(SIDE):
        for c in range(2):
            for x in range(SIDE):
                for y in range(SIDE):
                    x2, y2, z2, c2 = move(x, y, z, c)
                    target = ((z2 % SIDE) * 2 + c2) * SIDE * SIDE + (x2 % SIDE) * SIDE + y2 % SIDE
                    out.append(((z * 2 + c) * SIDE * SIDE + x * SIDE + y, target))
    return out


def first(step):
    return pairs(lambda x, y, z, c: (x + step, y, z, c) if c == 0 else (x, y + step, z, c))


def second(step):
    return pairs(lambda x, y, z, c: (x, y + step, z, c) if c == 0 else (x + step, y, z, c))


def along_z(step):
    return pairs(lambda x, y, z, c: (x, y, z + step, c))


OTHER = pairs(lambda x, y, z, c: (x, y, z, 1 - c))


def send(value, route):
    return lax.ppermute(value, AXES, route)


VMEM = pl.BlockSpec(memory_space=pltpu.VMEM)
SMEM = pl.BlockSpec(memory_space=pltpu.SMEM)
ANYWHERE = pl.BlockSpec(memory_space=pl.ANY)
HBM = pl.BlockSpec(memory_space=pltpu.HBM)


def noise_kernel(core_ref, chol_ref, noise_ref, mine_ref, others_ref, chol, noise, sems):
    levels, _, half = mine_ref.shape
    copies = []
    for l in range(levels):
        copies.append(pltpu.make_async_copy(chol_ref.at[l], chol.at[l], sems.at[l, 0]))
        copies.append(pltpu.make_async_copy(noise_ref.at[l], noise.at[l], sems.at[l, 1]))
    for copy in copies:
        copy.start()
    low = core_ref[0] == 0
    for l in range(levels):
        copies[2 * l].wait()
        copies[2 * l + 1].wait()
        product = jnp.dot(chol[l], noise[l], preferred_element_type=jnp.float32)
        mine_ref[l] = jnp.where(low, product[:, :half], product[:, half:])
        others_ref[l] = jnp.where(low, product[:, half:], product[:, :half])


def noise_call(core, chol, noise):
    levels, rows, columns = noise.shape
    shape = jax.ShapeDtypeStruct((levels, rows, columns // 2), jnp.float32)
    return pl.pallas_call(
        noise_kernel,
        out_shape=(shape, shape),
        in_specs=[SMEM, HBM, HBM],
        out_specs=(VMEM, VMEM),
        scratch_shapes=[
            pltpu.VMEM(chol.shape, jnp.bfloat16),
            pltpu.VMEM(noise.shape, jnp.bfloat16),
            pltpu.SemaphoreType.DMA((levels, 2)),
        ],
        compiler_params=pltpu.CompilerParams(vmem_limit_bytes=56 * 1024 * 1024),
        cost_estimate=pl.CostEstimate(
            flops=2 * levels * rows * rows * columns, bytes_accessed=levels * rows * rows * 4, transcendentals=0
        ),
    )(core, chol, noise)


def pick(which, part, sources, target):
    def tree(low, high):
        if high - low == 1:
            target[...] = sources[low][part]
            return
        middle = (low + high) // 2

        @pl.when(which < middle)
        def _():
            tree(low, middle)

        @pl.when(which >= middle)
        def _():
            tree(middle, high)

    tree(0, len(sources))


def stage_kernel(level, token_ref, own_f, other_f, factor, sems):
    copies = [
        pltpu.make_async_copy(ref.at[level], factor.at[j], sems.at[j]) for j, ref in enumerate((own_f, other_f))
    ]
    for copy in copies:
        copy.start()
    for copy in copies:
        copy.wait()


def stage_call(level, token, own_f, other_f):
    return pl.pallas_call(
        functools.partial(stage_kernel, level),
        out_shape=jax.ShapeDtypeStruct((2,) + own_f.shape[1:], own_f.dtype),
        in_specs=[ANYWHERE, HBM, HBM],
        out_specs=VMEM,
        scratch_shapes=[pltpu.SemaphoreType.DMA((2,))],
        compiler_params=pltpu.CompilerParams(vmem_limit_bytes=30 * 1024 * 1024),
        cost_estimate=pl.CostEstimate(
            flops=0, bytes_accessed=2 * own_f.size // own_f.shape[0] * 2, transcendentals=0
        ),
    )(token, own_f, other_f)


def level_kernel(level, count, where_ref, *refs):
    sources = refs[:count]
    mine_ref, theirs_ref, factor, out_ref, give_ref, picked = refs[count:]

    def step(t, carry):
        code = where_ref[level, t >> 3, t & 7]
        pick(code >> 3, code & 7, sources, picked.at[t >> 3, t & 7])
        return carry

    lax.fori_loop(0, 16, step, 0)
    for j, terms in enumerate((mine_ref, theirs_ref)):
        total = terms[level]
        for k in range(8):
            total += jnp.dot(factor[j, k], picked[j, k], preferred_element_type=jnp.float32)
        out_ref[j] = total.astype(out_ref.dtype)
    give_ref[...] = out_ref[1]


def level_call(level, where, sources, mine, theirs, factor):
    rows, columns = mine.shape[-2:]
    return pl.pallas_call(
        functools.partial(level_kernel, level, len(sources)),
        out_shape=(
            jax.ShapeDtypeStruct((2, rows, columns), jnp.bfloat16),
            jax.ShapeDtypeStruct((rows, columns), jnp.bfloat16),
        ),
        in_specs=[SMEM] + [VMEM] * (len(sources) + 3),
        out_specs=(VMEM, VMEM),
        scratch_shapes=[pltpu.VMEM((2, 8, rows, columns), jnp.bfloat16)],
        compiler_params=pltpu.CompilerParams(vmem_limit_bytes=24 * 1024 * 1024),
        cost_estimate=pl.CostEstimate(
            flops=2 * 16 * rows * rows * columns, bytes_accessed=16 * rows * columns * 2, transcendentals=0
        ),
    )(where, *sources, mine, theirs, factor)


def body(prior_draws, cond_factors, chol_factors, noise, neighbours, block_slot):
    my_gx = lax.axis_index("gx")
    my_gy = lax.axis_index("gy")
    z, core = my_gx // 2, my_gx % 2
    x, y = my_gy // SIDE, my_gy % SIDE
    half = prior_draws.shape[-1] // 2
    low = core == 0

    prior = prior_draws[0, 0]
    mine = jnp.where(low, prior[:, :half], prior[:, half:])
    others = jnp.where(low, prior[:, half:], prior[:, :half])
    draws = jnp.stack([mine, send(others, OTHER)])

    own_n = neighbours[:, 0, 0]
    both_n = jnp.stack([own_n, send(own_n, OTHER)], axis=1)

    device = block_slot[both_n] % (2 * SIDE**3)
    row, col = device // (SIDE * SIDE), device % (SIDE * SIDE)
    j = jnp.arange(2, dtype=jnp.int32)[None, :, None]
    my_row = z * 2 + jnp.where(j == 0, core, 1 - core)
    dx, dy = (col // SIDE - x) % SIDE, (col % SIDE - y) % SIDE
    dz = (row // 2 - z) % SIDE
    d1, d2 = jnp.where(low, dx, dy), jnp.where(low, dy, dx)

    def place(d):
        return jnp.where(d == 0, 0, jnp.where(d == 3, 1, jnp.where(d == 1, 2, 3)))

    p1, p2, p3 = place(d1), place(d2), place(dz)
    in_row = jnp.where(
        p2 == 0,
        p1 * 8 + j,
        jnp.where(
            p1 > 0,
            (SOON - 1 + p2) * 8 + (p1 - 1) * 2 + j,
            jnp.where(p2 < 3, (3 + p2) * 8 + j, (SOON + j) * 8 + 6),
        ),
    )
    in_col = jnp.where(p3 == 0, 0, 5 + p3) * 8 + jnp.where(row % 2 == core, 0, 1)
    own_far = (SOON - 1 + p2) * 8 + 6 + j
    in_row = jnp.concatenate([jnp.where((p1 == 0) & (p2 > 0), own_far, in_row)[:1], in_row[1:]])
    where = jnp.where(row == my_row, in_row, in_col).astype(jnp.int32)

    own_f = cond_factors[:, 0, 0]
    own_terms, sent_terms = noise_call(core.reshape(1), chol_factors[:, 0, 0], noise[:, 0, 0])

    kept, given, got = [], [], []
    for level in range(cond_factors.shape[0]):
        near = [send(draws, first(s)) for s in (2, 1, -1)]
        if level == 0:
            held, sent_terms, where = lax.optimization_barrier((draws, sent_terms, where))
            other_terms = send(sent_terms, OTHER)
            other_terms, held_f = lax.optimization_barrier((other_terms, own_f))
            other_f = send(held_f, OTHER)
        else:
            swapped = send(given[-1], OTHER)
            held, swapped = lax.optimization_barrier((draws, swapped))
            got.append(swapped)
        along = [send(held, second(s)) for s in (1, -1)] if level > 0 else [draws, draws]
        line = jnp.concatenate([near[1], near[2], near[0]])
        held, line = lax.optimization_barrier((held, line))
        if level == 0:
            whole_line = jnp.concatenate([line, held])
            far = [send(whole_line, second(s)) for s in (2, 1, -1)]
        else:
            far = [
                send(line, second(2)),
                send(jnp.concatenate([line, along[0][:1]]), second(1)),
                send(jnp.concatenate([line, along[1][1:]]), second(-1)),
            ]
        column = [send(held, along_z(s)) for s in (2, 1, -1)]
        factor = stage_call(level, line, own_f, other_f)
        sources = [draws, near[1], near[2], near[0]] + along + [column[1], column[2], column[0]]
        sources += [far[1], far[2], far[0]]
        draws, give = level_call(level, where, sources, own_terms, other_terms, factor)
        kept.append(draws[0])
        given.append(give)
    got.append(send(given[-1], OTHER))
    left = jnp.stack(kept)
    right = jnp.stack(got)
    whole = jnp.where(low, jnp.concatenate([left, right], axis=-1), jnp.concatenate([right, left], axis=-1))
    return whole[:, None, None]


def solution(mesh):
    in_specs = (
        P("gx", "gy", None, None),
        P(None, "gx", "gy", None, None, None),
        P(None, "gx", "gy", None, None),
        P(None, "gx", "gy", None, None),
        P(None, "gx", "gy", None),
        P(),
    )
    out_specs = P(None, "gx", "gy", None, None)
    return jax.shard_map(body, mesh=mesh, in_specs=in_specs, out_specs=out_specs, check_vma=False)
```

```python
import functools

import jax
import jax.numpy as jnp
from jax import lax
from jax.experimental import pallas as pl
from jax.experimental.pallas import tpu as pltpu
from jax.sharding import PartitionSpec as P

AXES = ("gx", "gy")
SIDE = 4
SOON = 9


def pairs(move):
    out = []
    for z in range(SIDE):
        for c in range(2):
            for x in range(SIDE):
                for y in range(SIDE):
                    x2, y2, z2, c2 = move(x, y, z, c)
                    target = ((z2 % SIDE) * 2 + c2) * SIDE * SIDE + (x2 % SIDE) * SIDE + y2 % SIDE
                    out.append(((z * 2 + c) * SIDE * SIDE + x * SIDE + y, target))
    return out


def first(step):
    return pairs(lambda x, y, z, c: (x + step, y, z, c) if c == 0 else (x, y + step, z, c))


def second(step):
    return pairs(lambda x, y, z, c: (x, y + step, z, c) if c == 0 else (x + step, y, z, c))


def along_z(step):
    return pairs(lambda x, y, z, c: (x, y, z + step, c))


OTHER = pairs(lambda x, y, z, c: (x, y, z, 1 - c))


def send(value, route):
    return lax.ppermute(value, AXES, route)


VMEM = pl.BlockSpec(memory_space=pltpu.VMEM)
SMEM = pl.BlockSpec(memory_space=pltpu.SMEM)
ANYWHERE = pl.BlockSpec(memory_space=pl.ANY)
HBM = pl.BlockSpec(memory_space=pltpu.HBM)


def noise_kernel(core_ref, chol_ref, noise_ref, mine_ref, others_ref, chol, noise, sems):
    levels, _, half = mine_ref.shape
    copies = []
    for l in range(levels):
        copies.append(pltpu.make_async_copy(chol_ref.at[l], chol.at[l], sems.at[l, 0]))
        copies.append(pltpu.make_async_copy(noise_ref.at[l], noise.at[l], sems.at[l, 1]))
    for copy in copies:
        copy.start()
    low = core_ref[0] == 0
    for l in range(levels):
        copies[2 * l].wait()
        copies[2 * l + 1].wait()
        product = jnp.dot(chol[l], noise[l], preferred_element_type=jnp.float32)
        mine_ref[l] = jnp.where(low, product[:, :half], product[:, half:])
        others_ref[l] = jnp.where(low, product[:, half:], product[:, :half])


def noise_call(core, chol, noise):
    levels, rows, columns = noise.shape
    shape = jax.ShapeDtypeStruct((levels, rows, columns // 2), jnp.float32)
    return pl.pallas_call(
        noise_kernel,
        out_shape=(shape, shape),
        in_specs=[SMEM, HBM, HBM],
        out_specs=(VMEM, VMEM),
        scratch_shapes=[
            pltpu.VMEM(chol.shape, jnp.bfloat16),
            pltpu.VMEM(noise.shape, jnp.bfloat16),
            pltpu.SemaphoreType.DMA((levels, 2)),
        ],
        compiler_params=pltpu.CompilerParams(vmem_limit_bytes=56 * 1024 * 1024),
        cost_estimate=pl.CostEstimate(
            flops=2 * levels * rows * rows * columns, bytes_accessed=levels * rows * rows * 4, transcendentals=0
        ),
    )(core, chol, noise)


def pick(which, part, sources, target):
    def tree(low, high):
        if high - low == 1:
            target[...] = sources[low][part]
            return
        middle = (low + high) // 2

        @pl.when(which < middle)
        def _():
            tree(low, middle)

        @pl.when(which >= middle)
        def _():
            tree(middle, high)

    tree(0, len(sources))


def stage_kernel(level, token_ref, own_f, other_f, factor, sems):
    copies = [
        pltpu.make_async_copy(ref.at[level], factor.at[j], sems.at[j]) for j, ref in enumerate((own_f, other_f))
    ]
    for copy in copies:
        copy.start()
    for copy in copies:
        copy.wait()


def stage_call(level, token, own_f, other_f):
    return pl.pallas_call(
        functools.partial(stage_kernel, level),
        out_shape=jax.ShapeDtypeStruct((2,) + own_f.shape[1:], own_f.dtype),
        in_specs=[ANYWHERE, HBM, HBM],
        out_specs=VMEM,
        scratch_shapes=[pltpu.SemaphoreType.DMA((2,))],
        compiler_params=pltpu.CompilerParams(vmem_limit_bytes=30 * 1024 * 1024),
        cost_estimate=pl.CostEstimate(
            flops=0, bytes_accessed=2 * own_f.size // own_f.shape[0] * 2, transcendentals=0
        ),
    )(token, own_f, other_f)


def level_kernel(level, count, where_ref, *refs):
    sources = refs[:count]
    mine_ref, theirs_ref, factor, out_ref, give_ref, picked = refs[count:]

    def step(t, carry):
        code = where_ref[level, t >> 3, t & 7]
        pick(code >> 3, code & 7, sources, picked.at[t >> 3, t & 7])
        return carry

    lax.fori_loop(0, 16, step, 0)
    for j, terms in enumerate((mine_ref, theirs_ref)):
        total = terms[level]
        for k in range(8):
            total += jnp.dot(factor[j, k], picked[j, k], preferred_element_type=jnp.float32)
        out_ref[j] = total.astype(out_ref.dtype)
    give_ref[...] = out_ref[1]


def level_call(level, where, sources, mine, theirs, factor):
    rows, columns = mine.shape[-2:]
    return pl.pallas_call(
        functools.partial(level_kernel, level, len(sources)),
        out_shape=(
            jax.ShapeDtypeStruct((2, rows, columns), jnp.bfloat16),
            jax.ShapeDtypeStruct((rows, columns), jnp.bfloat16),
        ),
        in_specs=[SMEM] + [VMEM] * (len(sources) + 3),
        out_specs=(VMEM, VMEM),
        scratch_shapes=[pltpu.VMEM((2, 8, rows, columns), jnp.bfloat16)],
        compiler_params=pltpu.CompilerParams(vmem_limit_bytes=24 * 1024 * 1024),
        cost_estimate=pl.CostEstimate(
            flops=8 * 16 * rows * rows * columns, bytes_accessed=16 * rows * columns * 2, transcendentals=0
        ),
    )(where, *sources, mine, theirs, factor)


def body(prior_draws, cond_factors, chol_factors, noise, neighbours, block_slot):
    my_gx = lax.axis_index("gx")
    my_gy = lax.axis_index("gy")
    z, core = my_gx // 2, my_gx % 2
    x, y = my_gy // SIDE, my_gy % SIDE
    half = prior_draws.shape[-1] // 2
    low = core == 0

    prior = prior_draws[0, 0]
    mine = jnp.where(low, prior[:, :half], prior[:, half:])
    others = jnp.where(low, prior[:, half:], prior[:, :half])
    draws = jnp.stack([mine, send(others, OTHER)])

    own_n = neighbours[:, 0, 0]
    both_n = jnp.stack([own_n, send(own_n, OTHER)], axis=1)

    device = block_slot[both_n] % (2 * SIDE**3)
    row, col = device // (SIDE * SIDE), device % (SIDE * SIDE)
    j = jnp.arange(2, dtype=jnp.int32)[None, :, None]
    my_row = z * 2 + jnp.where(j == 0, core, 1 - core)
    dx, dy = (col // SIDE - x) % SIDE, (col % SIDE - y) % SIDE
    dz = (row // 2 - z) % SIDE
    d1, d2 = jnp.where(low, dx, dy), jnp.where(low, dy, dx)

    def place(d):
        return jnp.where(d == 0, 0, jnp.where(d == 3, 1, jnp.where(d == 1, 2, 3)))

    p1, p2, p3 = place(d1), place(d2), place(dz)
    in_row = jnp.where(
        p2 == 0,
        p1 * 8 + j,
        jnp.where(
            p1 > 0,
            (SOON - 1 + p2) * 8 + (p1 - 1) * 2 + j,
            jnp.where(p2 < 3, (3 + p2) * 8 + j, (SOON + j) * 8 + 6),
        ),
    )
    in_col = jnp.where(p3 == 0, 0, 5 + p3) * 8 + jnp.where(row % 2 == core, 0, 1)
    own_far = (SOON - 1 + p2) * 8 + 6 + j
    in_row = jnp.concatenate([jnp.where((p1 == 0) & (p2 > 0), own_far, in_row)[:1], in_row[1:]])
    where = jnp.where(row == my_row, in_row, in_col).astype(jnp.int32)

    own_f = cond_factors[:, 0, 0]
    own_terms, sent_terms = noise_call(core.reshape(1), chol_factors[:, 0, 0], noise[:, 0, 0])

    kept, given, got = [], [], []
    for level in range(cond_factors.shape[0]):
        near = [send(draws, first(s)) for s in (2, 1, -1)]
        if level == 0:
            held, sent_terms, where = lax.optimization_barrier((draws, sent_terms, where))
            other_terms = send(sent_terms, OTHER)
            other_terms, held_f = lax.optimization_barrier((other_terms, own_f))
            other_f = send(held_f, OTHER)
        else:
            swapped = send(given[-1], OTHER)
            held, swapped = lax.optimization_barrier((draws, swapped))
            got.append(swapped)
        along = [send(held, second(s)) for s in (1, -1)] if level > 0 else [draws, draws]
        line = jnp.concatenate([near[1], near[2], near[0]])
        held, line = lax.optimization_barrier((held, line))
        if level == 0:
            whole_line = jnp.concatenate([line, held])
            far = [send(whole_line, second(s)) for s in (2, 1, -1)]
        else:
            far = [
                send(line, second(2)),
                send(jnp.concatenate([line, along[0][:1]]), second(1)),
                send(jnp.concatenate([line, along[1][1:]]), second(-1)),
            ]
        column = [send(held, along_z(s)) for s in (2, 1, -1)]
        factor = stage_call(level, line, own_f, other_f)
        sources = [draws, near[1], near[2], near[0]] + along + [column[1], column[2], column[0]]
        sources += [far[1], far[2], far[0]]
        draws, give = level_call(level, where, sources, own_terms, other_terms, factor)
        kept.append(draws[0])
        given.append(give)
    def joined(left, right):
        return jnp.where(low, jnp.concatenate([left, right], axis=-1), jnp.concatenate([right, left], axis=-1))

    levels = len(kept)
    whole = joined(jnp.stack(kept[:-1]), jnp.stack(got))
    whole = jnp.concatenate([whole, jnp.zeros_like(whole[:1])])
    last = joined(kept[-1], send(given[-1], OTHER))
    whole = lax.dynamic_update_slice(whole, last[None], (levels - 1, 0, 0))
    return whole[:, None, None]


def solution(mesh):
    in_specs = (
        P("gx", "gy", None, None),
        P(None, "gx", "gy", None, None, None),
        P(None, "gx", "gy", None, None),
        P(None, "gx", "gy", None, None),
        P(None, "gx", "gy", None),
        P(),
    )
    out_specs = P(None, "gx", "gy", None, None)
    return jax.shard_map(body, mesh=mesh, in_specs=in_specs, out_specs=out_specs, check_vma=False)
```
